256 devices in a mesh: row: 8 (over x, y_hi), col: 16 (over z, core), rep: 2 (over y_lo).
Axes of the slice: x: 4, y: 4 (y_hi: 2, y_lo: 2; y = y_hi * 2 + y_lo), z: 8, core: 2. Of those that a mesh axis runs over, the one named last changes fastest.
Arguments:
- grad_out: float32 [65536, 256], P(('row', 'col', 'rep')), may hold values from -6 to 6
- tile_vals: bfloat16 [98304, 128, 128], P(('row', 'col', 'rep')), may hold values from 0.0039978027 to 0.039794922
- tile_rows: int32 [98304], P(('row', 'col', 'rep')), may hold values from 0 to 63
- tile_cols: int32 [98304], P(('row', 'col', 'rep')), may hold values from 0 to 31
- tile_counts: int32 [256], P(('row', 'col', 'rep')), may hold values from 1 to 384, as said below
Outputs:
- grad_in: float32 [65536, 256], P(('col', 'row', 'rep'))
The draws below stay inside these ranges and needn't reach their ends.
Inputs may be any that keep to these rules, and one draw needn't show every extreme that they name: `tile_counts`: some tile list uses all 384 slots. `tile_rows`: positions may repeat within a list and between lists.
All inputs are finite; a program needn't handle non-finite values.
Results may differ from the reference program's by a relative error of at most 0.0029.
Values may be sent and summed in bfloat16 or wider, within the bound.
A program may use at most 128 MiB of HBM per device.

```python
import math
import jax
import jax.numpy as jnp
from jax import lax

D = 256
TILE = 128
MAXT = 384
GRID_DEVS = 256
ITEMS = 65536
ROWBLK = 8192
COLBLK = 4096
N_ROW = 8
N_COL = 16
N_REP = 2


def draw_tile_counts(key, part):
    key = jax.random.fold_in(key, 7)
    first_key, second_key, third_key = jax.random.split(key, 3)
    first = jax.random.randint(first_key, (GRID_DEVS,), 1, MAXT + 1, dtype=jnp.int32)
    second = jax.random.randint(second_key, (GRID_DEVS,), 1, MAXT + 1, dtype=jnp.int32)
    counts = jnp.maximum(first * second // MAXT, 1)
    busiest = jax.random.randint(third_key, (), 0, GRID_DEVS, dtype=jnp.int32)
    counts = counts.at[busiest].set(MAXT)
    return counts.astype(jnp.int32)


def touch_ends(entries, own_key, low, largest):
    longest = entries.shape.index(max(entries.shape))
    spots = []
    for shift in (0, 1):
        where = [jax.random.randint(jax.random.fold_in(own_key, axis), (), 0, length) for axis, length in enumerate(entries.shape)]
        where[longest] = (where[longest] + shift) % entries.shape[longest]
        spots.append(tuple(where))
    return entries.at[spots[0]].set(low).at[spots[1]].set(largest)


def steps_of(stream_key, dims, shards, least, high):
    def one(position, blocks):
        draws = jax.random.uniform(jax.random.fold_in(jax.random.fold_in(stream_key, 6), position), (blocks,), jnp.float32, least / len(shards), high / len(shards))
        return jnp.repeat(jnp.exp(draws), dims[position] // blocks).reshape((-1,) + (1,) * (len(dims) - position - 1))

    factor_of = one(*shards[0])
    for cut in shards[1:]:
        factor_of = factor_of * one(*cut)
    return factor_of


def normal_values(stream_key, extent, scale, most, shards=(), kind=jnp.bfloat16):
    values = jax.random.normal(stream_key, extent, jnp.float32) * scale
    if len(shards) > 0:
        values = steps_of(stream_key, extent, shards, -0.22, 0.18) * values
    return jnp.clip(values, min=-most, max=most).astype(kind)


def setup_inputs(seed: int = 0) -> dict:
    arg_keys = jax.random.split(jax.random.key(seed), 6)
    return {
        "grad_out": normal_values(arg_keys[0], (ITEMS, D), 1.0, 6.0, ((0, 256),), jnp.float32),
        "tile_vals": jnp.clip(jnp.exp(math.log(0.039794922) - 2.2979944 * jax.random.uniform(arg_keys[1], (GRID_DEVS * MAXT, TILE, TILE), jnp.float32) ** steps_of(arg_keys[1], (GRID_DEVS * MAXT, TILE, TILE), ((0, 256),), -0.2, 0.2)), 0.0039978027, 0.039794922).astype(jnp.bfloat16),
        "tile_rows": touch_ends(jax.random.randint(arg_keys[2], (GRID_DEVS * MAXT,), 0, ROWBLK // TILE), jax.random.fold_in(arg_keys[2], 1), 0, (ROWBLK // TILE) - 1).astype(jnp.int32),
        "tile_cols": touch_ends(jax.random.randint(arg_keys[3], (GRID_DEVS * MAXT,), 0, COLBLK // TILE), jax.random.fold_in(arg_keys[3], 1), 0, (COLBLK // TILE) - 1).astype(jnp.int32),
        "tile_counts": draw_tile_counts(jax.random.fold_in(arg_keys[5], 71), 0),
    }


def reference(grad_out, tile_vals, tile_rows, tile_cols, tile_counts):
    rounded = grad_out.astype(jnp.bfloat16)
    widened = lax.optimization_barrier(rounded).astype(jnp.float32)
    grad_tiles = widened.reshape(N_ROW, ROWBLK // TILE, TILE, D)
    tiles_all = tile_vals.reshape(GRID_DEVS, MAXT, TILE, TILE)
    rows_all = tile_rows.reshape(GRID_DEVS, MAXT)
    cols_all = tile_cols.reshape(GRID_DEVS, MAXT)
    slot_ids = jnp.arange(MAXT, dtype=jnp.int32)

    def one_list(totals, inputs):
        list_index, tiles, row_index, col_index, used_slots = inputs
        row_group = (list_index // (N_COL * N_REP)).astype(jnp.int32)
        col_group = ((list_index // N_REP) % N_COL).astype(jnp.int32)
        block = lax.dynamic_index_in_dim(grad_tiles, row_group, 0, keepdims=False)
        selected = jnp.take(block, row_index, axis=0)
        products = jnp.einsum("tij,tid->tjd", tiles.astype(jnp.float32), selected,
                              precision=lax.Precision.HIGHEST)
        products = jnp.where((slot_ids < used_slots)[:, None, None], products, jnp.zeros_like(products))
        totals = totals.at[col_group, col_index].add(products)
        return totals, None

    initial = jnp.zeros((N_COL, COLBLK // TILE, TILE, D), jnp.float32)
    totals, ignored = lax.scan(one_list, initial,
                               (jnp.arange(GRID_DEVS, dtype=jnp.int32), tiles_all, rows_all, cols_all, tile_counts))
    return totals.reshape(ITEMS, D)
```

```python
import functools

import jax
import jax.numpy as jnp
from jax import lax
from jax.experimental import pallas as pl
from jax.experimental.pallas import tpu as pltpu
from jax.sharding import PartitionSpec as P

MESH = pl.DeviceIdType.MESH
T = 128
D = 256
SLOTS = 384
PAIRS = 208
BATCH = 26
CHUNKS = (128, 128)
X, Y, Z = 4, 4, 8


def prepare(rows, cols, count, z, y):
    zs, cs, ys, ts = rows >> 3, (rows >> 2) & 1, (rows >> 1) & 1, rows & 1
    zrel = (zs - z + 8) & 7
    zslot = jnp.where(zrel < 4, 2 * zrel, jnp.where(zrel == 4, 7, 15 - 2 * zrel))
    yrel = (ys - y + 2) & 1
    place = jnp.where(cs == 0, yrel * 16 + zslot * 2 + ts, 32 + zslot * 4 + yrel * 2 + ts)

    lane = lax.broadcasted_iota(jnp.int32, (1, SLOTS), 1)
    colr = jnp.where(lane < count, cols, 64)

    def column(v):
        return jnp.transpose(jnp.broadcast_to(v, (T, SLOTS)))

    colc, placec = column(colr), column(place)
    slotc = lax.broadcasted_iota(jnp.int32, (SLOTS, T), 0)
    one, zero = jnp.int32(1), jnp.int32(0)
    lanes = lax.broadcasted_iota(jnp.int32, (SLOTS, T), 1)
    n_row = jnp.sum(jnp.where(colc == lanes, one, zero), axis=0, keepdims=True)
    pair_row = jnp.where(lax.broadcasted_iota(jnp.int32, (1, T), 1) < 32, (n_row + 1) >> 1, 0)
    pair_col = jnp.transpose(jnp.broadcast_to(pair_row, (T, T)))
    sub = lax.broadcasted_iota(jnp.int32, (T, T), 0)
    lan = lax.broadcasted_iota(jnp.int32, (T, T), 1)
    ends = jnp.sum(jnp.where(sub <= lan, pair_col, zero), axis=0, keepdims=True)
    starts = ends - pair_row
    last = jnp.where(pair_row > 0, ends - 1, PAIRS)
    wide = jnp.concatenate([colc] * (SLOTS // T), axis=1)
    si = lax.broadcasted_iota(jnp.int32, (SLOTS, SLOTS), 0)
    ti = lax.broadcasted_iota(jnp.int32, (SLOTS, SLOTS), 1)
    same = jnp.where((wide == colr) & (ti < si), 1.0, 0.0)
    rank = jnp.sum(same, axis=1, keepdims=True).astype(jnp.int32)
    mine = jnp.where(colc == lanes, jnp.broadcast_to(starts, (SLOTS, T)), zero)
    start = jnp.sum(mine.astype(jnp.float32), axis=1, keepdims=True).astype(jnp.int32)
    pos = jnp.where(colc[:, :1] < 32, 2 * start + rank, -1)
    opens = jnp.where(rank == 0, one, zero)
    parts = [[], [], []]
    for block in range(4):
        target = lanes + block * T
        hit = jnp.broadcast_to(pos, (SLOTS, T)) == target
        parts[0].append(SLOTS + jnp.sum(jnp.where(hit, slotc - SLOTS, zero), axis=0, keepdims=True))
        parts[1].append(jnp.sum(jnp.where(hit, placec, zero), axis=0, keepdims=True))
        parts[2].append(jnp.sum(jnp.where(hit, jnp.broadcast_to(opens, (SLOTS, T)), zero), axis=0, keepdims=True))
    out = [jnp.concatenate(p, axis=1) for p in parts]
    out.append(jnp.concatenate([last] * 4, axis=1))
    return jnp.concatenate(out + out, axis=0)


def kernel(grad_hbm, tiles_hbm, rows_hbm, cols_hbm, count_hbm, out_ref, *scratch):
    F = len(CHUNKS)
    it = iter(scratch)
    grad, rows, cols, count, tiles, table, meta, sums = (next(it) for _ in range(8))
    G = [next(it) for _ in range(F)]
    SB = [next(it) for _ in range(F)]
    R1 = [next(it) for _ in range(F)]
    SC = [next(it) for _ in range(F)]
    R2 = [next(it) for _ in range(F)]
    own = [next(it) for _ in range(F)]
    local, zsem, ysem, csem, gsend, s1, s2, rs1, rs2 = (next(it) for _ in range(9))

    row, col, rep = lax.axis_index("row"), lax.axis_index("col"), lax.axis_index("rep")
    x, y = row // 2, lax.rem(row, 2) * 2 + rep
    z, core = col // 2, lax.rem(col, 2)

    def device(x, y, z, core):
        return (x * 2 + y // 2, z * 2 + core, lax.rem(y, 2))

    up = device(x, y, lax.rem(z + 1, Z), core)
    down = device(x, y, lax.rem(z + Z - 1, Z), core)
    across = device(x, y + 1 - 2 * rep, z, core)
    sibling = device(x, y, z, 1 - core)
    along_x = [device(lax.rem(x + k, X), y, z, core) for k in range(1, X)]
    along_y = [device(x, lax.rem(y + k, Y), z, core) for k in range(1, Y)]

    barrier = pltpu.get_barrier_semaphore()
    for other in [up, down, sibling] + along_x + along_y:
        pl.semaphore_signal(barrier, inc=1, device_id=other, device_id_type=MESH)

    loads = [
        pltpu.make_async_copy(grad_hbm, grad, local.at[0]),
        pltpu.make_async_copy(rows_hbm, rows, local.at[1]),
        pltpu.make_async_copy(cols_hbm, cols, local.at[2]),
        pltpu.make_async_copy(count_hbm, count, local.at[3]),
        pltpu.make_async_copy(tiles_hbm, tiles.at[pl.ds(0, SLOTS)], local.at[4]),
    ]
    for load in loads:
        load.start()
    tiles[SLOTS] = jnp.zeros((T, T), jnp.bfloat16)
    sums[PAIRS] = jnp.zeros(sums.shape[1:], jnp.bfloat16)

    loads[0].wait()
    base = core * 32
    firsts = [sum(CHUNKS[:m]) for m in range(F)]
    for t in range(2):
        flipped = jnp.transpose(grad[t * T : (t + 1) * T, :]).astype(jnp.bfloat16)
        for m in range(F):
            G[m][base + t] = flipped[firsts[m] : firsts[m] + CHUNKS[m]]
    pl.semaphore_wait(barrier, 9)

    def tiles_to(m, start, stop, n, to, sem):
        return pltpu.make_async_remote_copy(
            src_ref=G[m].at[pl.ds(start, n)],
            dst_ref=G[m].at[pl.ds(stop, n)],
            send_sem=gsend.at[m],
            recv_sem=sem,
            device_id=to,
            device_id_type=MESH,
        )

    def z_send(m, which, k, c):
        to = up if which == 0 else down
        nxt = 7 if k in (5, 6) else (k + 2 if k else 1 + which)
        at, n = (2, 2) if c == 0 else (4, 4)
        off = 32 * c
        tiles_to(m, off + at * k, off + at * nxt, n, to, zsem.at[m, nxt]).start()

    def z_wait(m, k, c):
        n = 2 if c == 0 else 4
        at = 2 * k if c == 0 else 32 + 4 * k
        tiles_to(m, at, at, n, up, zsem.at[m, k]).wait_recv()

    def y_send(m, start, n):
        tiles_to(m, start, start + 16, n, across, ysem.at[m]).start()

    def c_send(m, start, n):
        tiles_to(m, start, start, n, sibling, csem.at[m]).start()

    def gather(m, e):
        def zero():
            if e == 0:
                z_send(m, 0, 0, 0)
                z_send(m, 1, 0, 0)
                y_send(m, 0, 2)
            elif e in (1, 2):
                z_wait(m, 2 * e - 1, 0)
                z_send(m, 0, 2 * e - 1, 0)
                z_wait(m, 2 * e, 0)
                z_send(m, 1, 2 * e, 0)
                y_send(m, 4 * e - 2, 4)
            elif e == 3:
                z_wait(m, 5, 0)
                z_send(m, 0, 5, 0)
                z_wait(m, 6, 0)
                y_send(m, 10, 4)
            elif e == 4:
                z_wait(m, 7, 0)
                y_send(m, 14, 2)
                c_send(m, 0, 16)
            elif e == 5:
                tiles_to(m, 16, 16, 16, across, ysem.at[m]).wait_recv()
                c_send(m, 16, 16)
            elif e == 6:
                tiles_to(m, 32, 32, 32, sibling, csem.at[m]).wait_recv()

        def one():
            if e == 0:
                tiles_to(m, 32, 34, 2, across, ysem.at[m]).start()
            elif e == 1:
                tiles_to(m, 34, 34, 2, across, ysem.at[m]).wait_recv()
                z_send(m, 0, 0, 1)
                z_send(m, 1, 0, 1)
            elif e in (2, 3):
                z_wait(m, 2 * e - 3, 1)
                z_send(m, 0, 2 * e - 3, 1)
                z_wait(m, 2 * e - 2, 1)
                z_send(m, 1, 2 * e - 2, 1)
            elif e == 4:
                z_wait(m, 6, 1)
                z_send(m, 1, 6, 1)
                z_wait(m, 5, 1)
                c_send(m, 32, 28)
            elif e == 5:
                z_wait(m, 7, 1)
                c_send(m, 60, 4)
            elif e == 6:
                tiles_to(m, 0, 0, 32, sibling, csem.at[m]).wait_recv()

        pl.when(core == 0)(zero)
        pl.when(core == 1)(one)

    def multiply(m, hooks):
        M = CHUNKS[m]

        def step(b, run):
            for at, todo in hooks.items():
                pl.when(b == at)(todo)
            products, opens = [], []
            for q in range(BATCH):
                s = 2 * (b * BATCH + q)
                left = jnp.concatenate([G[m][meta[1, s]], G[m][meta[1, s + 1]]], axis=1)
                right = jnp.concatenate([tiles[meta[0, s]], tiles[meta[0, s + 1]]], axis=0)
                products.append(jnp.dot(left, right, preferred_element_type=jnp.float32))
                opens.append(meta[2, s])
            for q in range(BATCH):
                run = jnp.where(opens[q] != 0, 0.0, run) + products[q]
                sums[b * BATCH + q, :M] = run.astype(jnp.bfloat16)
            return run

        lax.fori_loop(0, PAIRS // BATCH, step, jnp.zeros((M, T), jnp.float32))

    def ring(buf_from, buf_to, i, k, n, ssem, rsem, to):
        return pltpu.make_async_remote_copy(
            src_ref=buf_from.at[i],
            dst_ref=buf_to.at[n],
            send_sem=ssem,
            recv_sem=rsem,
            device_id=to,
            device_id_type=MESH,
        )

    order = (1, 0, 2)

    def reduce(m, e):
        M, H = CHUNKS[m], CHUNKS[m] // 2
        if e == 0:
            for c in range(32):
                v = sums[meta[3, c], :M]
                xd, yd, t = c // 8, c // 2 % 4, c % 2
                SB[m][xd, 2 * yd + t] = v[:H]
                SB[m][4 + yd, 2 * xd + t] = v[H:]
            for k in order:
                ring(SB[m], R1[m], lax.rem(x + k + 1, X), k, k, s1.at[m], rs1.at[m], along_x[k]).start()
                ring(SB[m], R1[m], 4 + lax.rem(y + k + 1, Y), k, 3 + k, s1.at[m], rs1.at[m], along_y[k]).start()
        elif e == 1:
            everything = pltpu.make_async_remote_copy(
                src_ref=R1[m], dst_ref=R1[m], send_sem=s1.at[m], recv_sem=rs1.at[m], device_id=up, device_id_type=MESH
            )
            everything.wait_recv()
            for side, me in ((0, x), (1, y)):
                total = SB[m][4 * side + me].astype(jnp.float32)
                for k in range(3):
                    total += R1[m][3 * side + k].astype(jnp.float32)
                for d in range(4):
                    SC[m][4 * side + d] = total[2 * d : 2 * d + 2].astype(jnp.bfloat16)
                mine = SB[m][4 * side + me, pl.ds(2 * (y if side == 0 else x), 2)].astype(jnp.float32)
                for k in range(3):
                    mine += R1[m][3 * side + k, pl.ds(2 * (y if side == 0 else x), 2)].astype(jnp.float32)
                own[m][side] = mine
            for k in order:
                ring(SC[m], R2[m], lax.rem(y + k + 1, Y), k, k, s2.at[m], rs2.at[m], along_y[k]).start()
                ring(SC[m], R2[m], 4 + lax.rem(x + k + 1, X), k, 3 + k, s2.at[m], rs2.at[m], along_x[k]).start()
        elif e == 2:
            everything = pltpu.make_async_remote_copy(
                src_ref=R2[m], dst_ref=R2[m], send_sem=s2.at[m], recv_sem=rs2.at[m], device_id=up, device_id_type=MESH
            )
            everything.wait_recv()
            for side in range(2):
                total = own[m][side]
                for k in range(3):
                    total += R2[m][3 * side + k].astype(jnp.float32)
                out_ref[:, pl.ds(firsts[m] + side * H, H), :] = total

    def sent(m):
        tiles_to(m, 0, 0, 62, up, csem.at[m]).wait_send()
        pltpu.make_async_remote_copy(
            src_ref=R1[m], dst_ref=R1[m], send_sem=s1.at[m], recv_sem=rs1.at[m], device_id=up, device_id_type=MESH
        ).wait_send()
        pltpu.make_async_remote_copy(
            src_ref=R2[m], dst_ref=R2[m], send_sem=s2.at[m], recv_sem=rs2.at[m], device_id=up, device_id_type=MESH
        ).wait_send()

    gather(0, 0)
    for load in loads[1:4]:
        load.wait()
    table[...] = prepare(rows[...], cols[...], count[0], z, rep)
    to_scalars = pltpu.make_async_copy(table, meta, local.at[5])
    to_scalars.start()
    for e in range(1, 6):
        gather(0, e)
        gather(1, e - 1)
    gather(0, 6)
    to_scalars.wait()
    loads[4].wait()
    multiply(0, {2: lambda: gather(1, 5)})
    reduce(0, 0)
    gather(1, 6)
    multiply(1, {6: lambda: reduce(0, 1)})
    reduce(1, 0)
    reduce(0, 2)
    reduce(1, 1)
    reduce(1, 2)
    for m in range(F):
        sent(m)


def body(grad_out, tile_vals, tile_rows, tile_cols, tile_counts):
    vmem, bf16 = pltpu.VMEM, jnp.bfloat16
    F = len(CHUNKS)
    anywhere = pl.BlockSpec(memory_space=pl.ANY)
    shares = pl.pallas_call(
        kernel,
        out_shape=jax.ShapeDtypeStruct((2, D, T), jnp.float32),
        in_specs=[anywhere] * 5,
        out_specs=pl.BlockSpec(memory_space=vmem),
        scratch_shapes=[
            vmem((D, D), jnp.float32),
            vmem((1, SLOTS), jnp.int32),
            vmem((1, SLOTS), jnp.int32),
            pltpu.SMEM((1,), jnp.int32),
            vmem((SLOTS + 1, T, T), bf16),
            vmem((8, 512), jnp.int32),
            pltpu.SMEM((8, 512), jnp.int32),
            vmem((PAIRS + 1, max(CHUNKS), T), bf16),
        ]
        + [vmem((64, M, T), bf16) for M in CHUNKS]
        + [vmem((8, 8, M // 2, T), bf16) for M in CHUNKS]
        + [vmem((6, 8, M // 2, T), bf16) for M in CHUNKS]
        + [vmem((8, 2, M // 2, T), bf16) for M in CHUNKS]
        + [vmem((6, 2, M // 2, T), bf16) for M in CHUNKS]
        + [vmem((2, 2, M // 2, T), jnp.float32) for M in CHUNKS]
        + [
            pltpu.SemaphoreType.DMA((6,)),
            pltpu.SemaphoreType.DMA((F, 8)),
        ]
        + [pltpu.SemaphoreType.DMA((F,)) for _ in range(7)],
        compiler_params=pltpu.CompilerParams(
            collective_id=0, has_side_effects=True, vmem_limit_bytes=56 * 2**20
        ),
    )(grad_out, tile_vals, tile_rows.reshape(1, SLOTS), tile_cols.reshape(1, SLOTS), tile_counts)
    return jnp.transpose(shares, (0, 2, 1)).reshape(2 * T, D)


def solution(mesh):
    placed = (
        P(("row", "col", "rep"), None),
        P(("row", "col", "rep"), None, None),
        P(("row", "col", "rep")),
        P(("row", "col", "rep")),
        P(("row", "col", "rep")),
    )
    return jax.shard_map(
        body, mesh=mesh, in_specs=placed, out_specs=P(("col", "row", "rep"), None), check_vma=False
    )
```

```python
import functools

import jax
import jax.numpy as jnp
from jax import lax
from jax.experimental import pallas as pl
from jax.experimental.pallas import tpu as pltpu
from jax.sharding import PartitionSpec as P

MESH = pl.DeviceIdType.MESH
T = 128
D = 256
SLOTS = 384
PAIRS = 208
BATCH = 52
CHUNKS = (64, 64, 64, 64)
PLAN = [('g', 0, 0), ('g', 1, 0), ('g', 2, 0), ('g', 3, 0), ('p', 0, 0), ('g', 0, 1), ('g', 1, 1), ('g', 2, 1), ('g', 3, 1), ('g', 0, 2), ('g', 1, 2), ('g', 2, 2), ('g', 3, 2), ('g', 0, 3), ('g', 1, 3), ('g', 2, 3), ('g', 3, 3), ('g', 0, 4), ('g', 1, 4), ('g', 2, 4), ('g', 3, 4), ('g', 0, 5), ('g', 1, 5), ('g', 2, 5), ('g', 3, 5), ('g', 0, 6), ('w', 0, 0), ('m', 0, []), ('r', 0, 0), ('g', 1, 6), ('m', 1, []), ('r', 1, 0), ('g', 2, 6), ('m', 2, [(2, ('r', 0, 1))]), ('r', 2, 0), ('g', 3, 6), ('m', 3, [(2, ('r', 1, 1)), (3, ('r', 0, 2))]), ('r', 3, 0), ('r', 2, 1), ('r', 1, 2), ('r', 3, 1), ('r', 2, 2), ('r', 3, 2)]
X, Y, Z = 4, 4, 8


def prepare(rows, cols, count, z, y):
    zs, cs, ys, ts = rows >> 3, (rows >> 2) & 1, (rows >> 1) & 1, rows & 1
    zrel = (zs - z + 8) & 7
    zslot = jnp.where(zrel < 4, 2 * zrel, jnp.where(zrel == 4, 7, 15 - 2 * zrel))
    yrel = (ys - y + 2) & 1
    place = jnp.where(cs == 0, yrel * 16 + zslot * 2 + ts, 32 + zslot * 4 + yrel * 2 + ts)

    lane = lax.broadcasted_iota(jnp.int32, (1, SLOTS), 1)
    colr = jnp.where(lane < count, cols, 64)

    def column(v):
        return jnp.transpose(jnp.broadcast_to(v, (T, SLOTS)))

    colc, placec = column(colr), column(place)
    slotc = lax.broadcasted_iota(jnp.int32, (SLOTS, T), 0)
    one, zero = jnp.int32(1), jnp.int32(0)
    lanes = lax.broadcasted_iota(jnp.int32, (SLOTS, T), 1)
    n_row = jnp.sum(jnp.where(colc == lanes, one, zero), axis=0, keepdims=True)
    pair_row = jnp.where(lax.broadcasted_iota(jnp.int32, (1, T), 1) < 32, (n_row + 1) >> 1, 0)
    pair_col = jnp.transpose(jnp.broadcast_to(pair_row, (T, T)))
    sub = lax.broadcasted_iota(jnp.int32, (T, T), 0)
    lan = lax.broadcasted_iota(jnp.int32, (T, T), 1)
    ends = jnp.sum(jnp.where(sub <= lan, pair_col, zero), axis=0, keepdims=True)
    starts = ends - pair_row
    last = jnp.where(pair_row > 0, ends - 1, PAIRS)
    wide = jnp.concatenate([colc] * (SLOTS // T), axis=1)
    si = lax.broadcasted_iota(jnp.int32, (SLOTS, SLOTS), 0)
    ti = lax.broadcasted_iota(jnp.int32, (SLOTS, SLOTS), 1)
    same = jnp.where((wide == colr) & (ti < si), 1.0, 0.0)
    rank = jnp.sum(same, axis=1, keepdims=True).astype(jnp.int32)
    mine = jnp.where(colc == lanes, jnp.broadcast_to(starts, (SLOTS, T)), zero)
    start = jnp.sum(mine.astype(jnp.float32), axis=1, keepdims=True).astype(jnp.int32)
    pos = jnp.where(colc[:, :1] < 32, 2 * start + rank, -1)
    opens = jnp.where(rank == 0, one, zero)
    parts = [[], [], []]
    for block in range(4):
        target = lanes + block * T
        hit = jnp.broadcast_to(pos, (SLOTS, T)) == target
        parts[0].append(SLOTS + jnp.sum(jnp.where(hit, slotc - SLOTS, zero), axis=0, keepdims=True))
        parts[1].append(jnp.sum(jnp.where(hit, placec, zero), axis=0, keepdims=True))
        parts[2].append(jnp.sum(jnp.where(hit, jnp.broadcast_to(opens, (SLOTS, T)), zero), axis=0, keepdims=True))
    out = [jnp.concatenate(p, axis=1) for p in parts]
    out.append(jnp.concatenate([last] * 4, axis=1))
    return jnp.concatenate(out + out, axis=0)


def kernel(grad_hbm, tiles_hbm, rows_hbm, cols_hbm, count_hbm, out_ref, *scratch):
    F = len(CHUNKS)
    it = iter(scratch)
    grad, rows, cols, count, tiles, table, meta, sums = (next(it) for _ in range(8))
    G = [next(it) for _ in range(F)]
    SB = [next(it) for _ in range(F)]
    R1 = [next(it) for _ in range(F)]
    SC = [next(it) for _ in range(F)]
    R2 = [next(it) for _ in range(F)]
    own = [next(it) for _ in range(F)]
    local, zsem, ysem, csem, gsend, s1, s2, rs1, rs2 = (next(it) for _ in range(9))

    row, col, rep = lax.axis_index("row"), lax.axis_index("col"), lax.axis_index("rep")
    x, y = row // 2, lax.rem(row, 2) * 2 + rep
    z, core = col // 2, lax.rem(col, 2)

    def device(x, y, z, core):
        return (x * 2 + y // 2, z * 2 + core, lax.rem(y, 2))

    up = device(x, y, lax.rem(z + 1, Z), core)
    down = device(x, y, lax.rem(z + Z - 1, Z), core)
    across = device(x, y + 1 - 2 * rep, z, core)
    sibling = device(x, y, z, 1 - core)
    diagonal = device(x, y + 1 - 2 * rep, z, 1 - core)
    along_x = [device(lax.rem(x + k, X), y, z, core) for k in range(1, X)]
    along_y = [device(x, lax.rem(y + k, Y), z, core) for k in range(1, Y)]

    barrier = pltpu.get_barrier_semaphore()
    for other in [up, down, sibling, diagonal] + along_x + along_y:
        pl.semaphore_signal(barrier, inc=1, device_id=other, device_id_type=MESH)

    loads = [
        pltpu.make_async_copy(grad_hbm, grad, local.at[0]),
        pltpu.make_async_copy(rows_hbm, rows, local.at[1]),
        pltpu.make_async_copy(cols_hbm, cols, local.at[2]),
        pltpu.make_async_copy(count_hbm, count, local.at[3]),
        pltpu.make_async_copy(tiles_hbm, tiles.at[pl.ds(0, SLOTS)], local.at[4]),
    ]
    for load in loads:
        load.start()
    tiles[SLOTS] = jnp.zeros((T, T), jnp.bfloat16)
    sums[PAIRS] = jnp.zeros(sums.shape[1:], jnp.bfloat16)

    loads[0].wait()
    base = core * 32
    firsts = [sum(CHUNKS[:m]) for m in range(F)]
    for t in range(2):
        flipped = jnp.transpose(grad[t * T : (t + 1) * T, :]).astype(jnp.bfloat16)
        for m in range(F):
            G[m][base + t] = flipped[firsts[m] : firsts[m] + CHUNKS[m]]
    pl.semaphore_wait(barrier, 10)

    def tiles_to(m, start, stop, n, to, sem):
        return pltpu.make_async_remote_copy(
            src_ref=G[m].at[pl.ds(start, n)],
            dst_ref=G[m].at[pl.ds(stop, n)],
            send_sem=gsend.at[m],
            recv_sem=sem,
            device_id=to,
            device_id_type=MESH,
        )

    def z_send(m, which, k, c):
        to = up if which == 0 else down
        nxt = 7 if k in (5, 6) else (k + 2 if k else 1 + which)
        at, n = (2, 2) if c == 0 else (4, 4)
        off = 32 * c
        tiles_to(m, off + at * k, off + at * nxt, n, to, zsem.at[m, nxt]).start()

    def z_wait(m, k, c):
        n = 2 if c == 0 else 4
        at = 2 * k if c == 0 else 32 + 4 * k
        tiles_to(m, at, at, n, up, zsem.at[m, k]).wait_recv()

    def y_send(m, start, n, part=0):
        tiles_to(m, start, start + 16, n, across, ysem.at[m, part]).start()

    def c_send(m, start, n):
        tiles_to(m, start, start, n, sibling, csem.at[m]).start()

    def gather(m, e):
        def zero():
            if e == 0:
                z_send(m, 0, 0, 0)
                z_send(m, 1, 0, 0)
                y_send(m, 0, 2)
            elif e in (1, 2):
                z_wait(m, 2 * e - 1, 0)
                z_send(m, 0, 2 * e - 1, 0)
                z_wait(m, 2 * e, 0)
                z_send(m, 1, 2 * e, 0)
                y_send(m, 4 * e - 2, 4)
            elif e == 3:
                z_wait(m, 5, 0)
                z_send(m, 0, 5, 0)
                z_wait(m, 6, 0)
                y_send(m, 10, 4)
            elif e == 4:
                z_wait(m, 7, 0)
                y_send(m, 14, 2, 1)
                tiles_to(m, 14, 30, 2, diagonal, csem.at[m]).start()
                c_send(m, 0, 16)
            elif e == 5:
                tiles_to(m, 16, 16, 14, across, ysem.at[m, 0]).wait_recv()
                c_send(m, 16, 14)
            elif e == 6:
                tiles_to(m, 30, 30, 2, across, ysem.at[m, 1]).wait_recv()
                tiles_to(m, 32, 32, 32, sibling, csem.at[m]).wait_recv()

        def one():
            if e == 0:
                tiles_to(m, 32, 34, 2, across, ysem.at[m, 0]).start()
                tiles_to(m, 32, 36, 2, up, zsem.at[m, 1]).start()
                tiles_to(m, 32, 40, 2, down, zsem.at[m, 2]).start()
            elif e == 1:
                tiles_to(m, 34, 34, 2, across, ysem.at[m, 0]).wait_recv()
                tiles_to(m, 34, 38, 2, up, zsem.at[m, 1]).start()
                tiles_to(m, 34, 42, 2, down, zsem.at[m, 2]).start()
            elif e in (2, 3):
                z_wait(m, 2 * e - 3, 1)
                z_send(m, 0, 2 * e - 3, 1)
                z_wait(m, 2 * e - 2, 1)
                z_send(m, 1, 2 * e - 2, 1)
            elif e == 4:
                z_wait(m, 6, 1)
                z_send(m, 1, 6, 1)
                z_wait(m, 5, 1)
                c_send(m, 32, 28)
            elif e == 5:
                z_wait(m, 7, 1)
                c_send(m, 60, 4)
            elif e == 6:
                tiles_to(m, 0, 0, 32, sibling, csem.at[m]).wait_recv()

        pl.when(core == 0)(zero)
        pl.when(core == 1)(one)

    def multiply(m, hooks):
        M = CHUNKS[m]

        def step(b, run):
            for at, todo in hooks.items():

                @pl.when(b == at)
                def _():
                    for item in todo:
                        do(item)

            products, opens = [], []
            for q in range(BATCH):
                s = 2 * (b * BATCH + q)
                left = jnp.concatenate([G[m][meta[1, s]], G[m][meta[1, s + 1]]], axis=1)
                right = jnp.concatenate([tiles[meta[0, s]], tiles[meta[0, s + 1]]], axis=0)
                products.append(jnp.dot(left, right, preferred_element_type=jnp.float32))
                opens.append(meta[2, s])
            for q in range(BATCH):
                run = jnp.where(opens[q] != 0, 0.0, run) + products[q]
                sums[b * BATCH + q, :M] = run.astype(jnp.bfloat16)
            return run

        lax.fori_loop(0, PAIRS // BATCH, step, jnp.zeros((M, T), jnp.float32))

    def whole(ref, ssem, rsem):
        return pltpu.make_async_remote_copy(
            src_ref=ref, dst_ref=ref, send_sem=ssem, recv_sem=rsem, device_id=up, device_id_type=MESH
        )

    def hop(src, dst, ssem, rsem, to):
        return pltpu.make_async_remote_copy(
            src_ref=src, dst_ref=dst, send_sem=ssem, recv_sem=rsem, device_id=to, device_id_type=MESH
        )

    sides = ((0, x, along_x, y, along_y), (1, y, along_y, x, along_x))

    def reduce(m, e):
        M, H = CHUNKS[m], CHUNKS[m] // 2
        if e == 0:
            for c in range(32):
                v = sums[meta[3, c], :M]
                xd, yd, t = c // 8, c // 2 % 4, c % 2
                SB[m][xd, 2 * yd + t] = v[:H]
                SB[m][4 + yd, 2 * xd + t] = v[H:]
            for k in (1, 0, 2):
                for side, me, along, _, _ in sides:
                    block = 4 * side + lax.rem(me + k + 1, 4)
                    hop(SB[m].at[block], R1[m].at[3 * side + k], s1.at[m], rs1.at[m], along[k]).start()
        elif e == 1:
            whole(R1[m], s1.at[m], rs1.at[m]).wait_recv()
            for side, me, _, place, _ in sides:
                total = SB[m][4 * side + me].astype(jnp.float32)
                for k in range(3):
                    total += R1[m][3 * side + k].astype(jnp.float32)
                for d in range(4):
                    SC[m][4 * side + d] = total[2 * d : 2 * d + 2].astype(jnp.bfloat16)
                at = pl.ds(2 * place, 2)
                mine = SB[m][4 * side + me, at].astype(jnp.float32)
                for k in range(3):
                    mine += R1[m][3 * side + k, at].astype(jnp.float32)
                own[m][side] = mine
            for k in (1, 0, 2):
                for side, _, _, place, along in sides:
                    block = 4 * side + lax.rem(place + k + 1, 4)
                    hop(SC[m].at[block], R2[m].at[3 * side + k], s2.at[m], rs2.at[m], along[k]).start()
        elif e == 2:
            whole(R2[m], s2.at[m], rs2.at[m]).wait_recv()
            for side in range(2):
                total = own[m][side]
                for k in range(3):
                    total += R2[m][3 * side + k].astype(jnp.float32)
                out_ref[:, pl.ds(firsts[m] + side * H, H), :] = total

    def sent(m):
        tiles_to(m, 0, 0, 62, up, csem.at[m]).wait_send()
        whole(R1[m], s1.at[m], rs1.at[m]).wait_send()
        whole(R2[m], s2.at[m], rs2.at[m]).wait_send()

    def do(item):
        kind, m, e = item
        if kind == "g":
            gather(m, e)
        elif kind == "r":
            reduce(m, e)
        elif kind == "p":
            for load in loads[1:4]:
                load.wait()
            table[...] = prepare(rows[...].reshape(1, SLOTS), cols[...].reshape(1, SLOTS), count[0], z, rep)
            to_scalars.start()
        elif kind == "w":
            to_scalars.wait()
            loads[4].wait()
        else:
            hooks = {}
            for at, what in e:
                hooks.setdefault(at, []).append(what)
            multiply(m, hooks)

    to_scalars = pltpu.make_async_copy(table, meta, local.at[5])
    for item in PLAN:
        do(item)
    for m in range(F):
        sent(m)


def body(grad_out, tile_vals, tile_rows, tile_cols, tile_counts):
    vmem, bf16 = pltpu.VMEM, jnp.bfloat16
    F = len(CHUNKS)
    anywhere = pl.BlockSpec(memory_space=pl.ANY)
    shares = pl.pallas_call(
        kernel,
        out_shape=jax.ShapeDtypeStruct((2, D, T), jnp.float32),
        in_specs=[anywhere] * 5,
        out_specs=pl.BlockSpec(memory_space=vmem),
        scratch_shapes=[
            vmem((D, D), jnp.float32),
            vmem((SLOTS,), jnp.int32),
            vmem((SLOTS,), jnp.int32),
            pltpu.SMEM((1,), jnp.int32),
            vmem((SLOTS + 1, T, T), bf16),
            vmem((8, 512), jnp.int32),
            pltpu.SMEM((8, 512), jnp.int32),
            vmem((PAIRS + 1, max(CHUNKS), T), bf16),
        ]
        + [vmem((64, M, T), bf16) for M in CHUNKS]
        + [vmem((8, 8, M // 2, T), bf16) for M in CHUNKS]
        + [vmem((6, 8, M // 2, T), bf16) for M in CHUNKS]
        + [vmem((8, 2, M // 2, T), bf16) for M in CHUNKS]
        + [vmem((6, 2, M // 2, T), bf16) for M in CHUNKS]
        + [vmem((2, 2, M // 2, T), jnp.float32) for M in CHUNKS]
        + [
            pltpu.SemaphoreType.DMA((6,)),
            pltpu.SemaphoreType.DMA((F, 8)),
            pltpu.SemaphoreType.DMA((F, 2)),
        ]
        + [pltpu.SemaphoreType.DMA((F,)) for _ in range(6)],
        compiler_params=pltpu.CompilerParams(
            collective_id=0, has_side_effects=True, vmem_limit_bytes=56 * 2**20
        ),
    )(grad_out, tile_vals, tile_rows, tile_cols, tile_counts)
    return jnp.transpose(shares, (0, 2, 1)).reshape(2 * T, D)


def solution(mesh):
    placed = (
        P(("row", "col", "rep"), None),
        P(("row", "col", "rep"), None, None),
        P(("row", "col", "rep")),
        P(("row", "col", "rep")),
        P(("row", "col", "rep")),
    )
    return jax.shard_map(
        body, mesh=mesh, in_specs=placed, out_specs=P(("col", "row", "rep"), None), check_vma=False
    )
```

```python
import functools

import jax
import jax.numpy as jnp
from jax import lax
from jax.experimental import pallas as pl
from jax.experimental.pallas import tpu as pltpu
from jax.sharding import PartitionSpec as P

MESH = pl.DeviceIdType.MESH
T = 128
D = 256
SLOTS = 384
PAIRS = 208
BATCH = 104
CHUNKS = (64, 96, 96)
PLAN = (
    [("g", 0, 0), ("o", 1, 0), ("g", 1, 0), ("g", 2, 0)]
    + [("g", 0, 1), ("g", 1, 1), ("g", 2, 1), ("t", 0, 0)]
    + [("g", 0, 2), ("g", 1, 2), ("g", 2, 2), ("p", 0, 0)]
    + [("g", 0, 3), ("g", 1, 3), ("g", 2, 3)]
    + [("g", 0, 4), ("g", 1, 4), ("g", 0, 5), ("g", 2, 4), ("w", 0, 0), ("g", 0, 6)]
    + [("m", 0, [(0, ("g", 1, 5)), (1, ("g", 2, 5))]), ("r", 0, 0), ("g", 1, 6)]
    + [("m", 1, []), ("r", 1, 0), ("g", 2, 6)]
    + [("m", 2, [(1, ("r", 0, 1))]), ("r", 2, 0)]
    + [("r", 0, 2), ("r", 1, 1), ("r", 2, 1), ("r", 1, 2), ("r", 2, 2)]
)
X, Y, Z = 4, 4, 8


def prepare(rows, cols, count, z, y):
    zs, cs, ys, ts = rows >> 3, (rows >> 2) & 1, (rows >> 1) & 1, rows & 1
    zrel = (zs - z + 8) & 7
    zslot = jnp.where(zrel < 4, 2 * zrel, jnp.where(zrel == 4, 7, 15 - 2 * zrel))
    yrel = (ys - y + 2) & 1
    place = jnp.where(cs == 0, yrel * 16 + zslot * 2 + ts, 32 + zslot * 4 + yrel * 2 + ts)

    lane = lax.broadcasted_iota(jnp.int32, (1, SLOTS), 1)
    colr = jnp.where(lane < count, cols, 64)

    def column(v):
        return jnp.transpose(jnp.broadcast_to(v, (T, SLOTS)))

    colc, placec = column(colr), column(place)
    slotc = lax.broadcasted_iota(jnp.int32, (SLOTS, T), 0)
    one, zero = jnp.int32(1), jnp.int32(0)
    lanes = lax.broadcasted_iota(jnp.int32, (SLOTS, T), 1)
    n_row = jnp.sum(jnp.where(colc == lanes, one, zero), axis=0, keepdims=True)
    pair_row = jnp.where(lax.broadcasted_iota(jnp.int32, (1, T), 1) < 32, (n_row + 1) >> 1, 0)
    pair_col = jnp.transpose(jnp.broadcast_to(pair_row, (T, T)))
    sub = lax.broadcasted_iota(jnp.int32, (T, T), 0)
    lan = lax.broadcasted_iota(jnp.int32, (T, T), 1)
    ends = jnp.sum(jnp.where(sub <= lan, pair_col, zero), axis=0, keepdims=True)
    starts = ends - pair_row
    last = jnp.where(pair_row > 0, ends - 1, PAIRS)
    wide = jnp.concatenate([colc] * (SLOTS // T), axis=1)
    si = lax.broadcasted_iota(jnp.int32, (SLOTS, SLOTS), 0)
    ti = lax.broadcasted_iota(jnp.int32, (SLOTS, SLOTS), 1)
    same = jnp.where((wide == colr) & (ti < si), 1.0, 0.0)
    rank = jnp.sum(same, axis=1, keepdims=True).astype(jnp.int32)
    mine = jnp.where(colc == lanes, jnp.broadcast_to(starts, (SLOTS, T)), zero)
    start = jnp.sum(mine.astype(jnp.float32), axis=1, keepdims=True).astype(jnp.int32)
    pos = jnp.where(colc[:, :1] < 32, 2 * start + rank, -1)
    opens = jnp.where(rank == 0, one, zero)
    parts = [[], [], []]
    for block in range(4):
        target = lanes + block * T
        hit = jnp.broadcast_to(pos, (SLOTS, T)) == target
        parts[0].append(SLOTS + jnp.sum(jnp.where(hit, slotc - SLOTS, zero), axis=0, keepdims=True))
        parts[1].append(jnp.sum(jnp.where(hit, placec, zero), axis=0, keepdims=True))
        parts[2].append(jnp.sum(jnp.where(hit, jnp.broadcast_to(opens, (SLOTS, T)), zero), axis=0, keepdims=True))
    out = [jnp.concatenate(p, axis=1) for p in parts]
    out.append(jnp.concatenate([last] * 4, axis=1))
    return jnp.concatenate(out + out, axis=0)


def kernel(grad_hbm, tiles_hbm, rows_hbm, cols_hbm, count_hbm, out_ref, *scratch):
    F = len(CHUNKS)
    it = iter(scratch)
    grad, rows, cols, count, tiles, table, meta, sums = (next(it) for _ in range(8))
    G = [next(it) for _ in range(F)]
    SB = [next(it) for _ in range(F)]
    R1 = [next(it) for _ in range(F)]
    SC = [next(it) for _ in range(F)]
    R2 = [next(it) for _ in range(F)]
    own = [next(it) for _ in range(F)]
    local, zsem, ysem, csem, gsend, s1, s2, rs1, rs2 = (next(it) for _ in range(9))

    row, col, rep = lax.axis_index("row"), lax.axis_index("col"), lax.axis_index("rep")
    x, y = row // 2, lax.rem(row, 2) * 2 + rep
    z, core = col // 2, lax.rem(col, 2)

    def device(x, y, z, core):
        return (x * 2 + y // 2, z * 2 + core, lax.rem(y, 2))

    up = device(x, y, lax.rem(z + 1, Z), core)
    down = device(x, y, lax.rem(z + Z - 1, Z), core)
    across = device(x, y + 1 - 2 * rep, z, core)
    sibling = device(x, y, z, 1 - core)
    diagonal = device(x, y + 1 - 2 * rep, z, 1 - core)
    along_x = [device(lax.rem(x + k, X), y, z, core) for k in range(1, X)]
    along_y = [device(x, lax.rem(y + k, Y), z, core) for k in range(1, Y)]

    barrier = pltpu.get_barrier_semaphore()
    for other in [up, down, sibling, diagonal] + along_x + along_y:
        pl.semaphore_signal(barrier, inc=1, device_id=other, device_id_type=MESH)

    loads = [
        pltpu.make_async_copy(grad_hbm.at[:, pl.ds(0, T)], grad.at[:, pl.ds(0, T)], local.at[0]),
        pltpu.make_async_copy(rows_hbm, rows, local.at[1]),
        pltpu.make_async_copy(cols_hbm, cols, local.at[2]),
        pltpu.make_async_copy(count_hbm, count, local.at[3]),
        pltpu.make_async_copy(tiles_hbm, tiles.at[pl.ds(0, SLOTS)], local.at[4]),
        pltpu.make_async_copy(grad_hbm.at[:, pl.ds(T, T)], grad.at[:, pl.ds(T, T)], local.at[6]),
    ]
    for i in (0, 5, 1, 2, 3):
        loads[i].start()
    tiles[SLOTS] = jnp.zeros((T, T), jnp.bfloat16)
    sums[PAIRS] = jnp.zeros(sums.shape[1:], jnp.bfloat16)

    base = core * 32
    firsts = [sum(CHUNKS[:m]) for m in range(F)]

    def own_part(half):
        loads[5 * half].wait()
        for t in range(2):
            flipped = jnp.transpose(grad[t * T : (t + 1) * T, half * T : (half + 1) * T]).astype(jnp.bfloat16)
            for m in range(F):
                start, stop = max(firsts[m], half * T), min(firsts[m] + CHUNKS[m], half * T + T)
                if start < stop:
                    G[m][base + t, start - firsts[m] : stop - firsts[m]] = flipped[start - half * T : stop - half * T]

    own_part(0)
    pl.semaphore_wait(barrier, 10)

    def tiles_to(m, start, stop, n, to, sem):
        return pltpu.make_async_remote_copy(
            src_ref=G[m].at[pl.ds(start, n)],
            dst_ref=G[m].at[pl.ds(stop, n)],
            send_sem=gsend.at[m],
            recv_sem=sem,
            device_id=to,
            device_id_type=MESH,
        )

    def z_send(m, which, k, c):
        to = up if which == 0 else down
        nxt = 7 if k in (5, 6) else (k + 2 if k else 1 + which)
        at, n = (2, 2) if c == 0 else (4, 4)
        off = 32 * c
        tiles_to(m, off + at * k, off + at * nxt, n, to, zsem.at[m, nxt]).start()

    def z_wait(m, k, c):
        n = 2 if c == 0 else 4
        at = 2 * k if c == 0 else 32 + 4 * k
        tiles_to(m, at, at, n, up, zsem.at[m, k]).wait_recv()

    def y_send(m, start, n, part=0):
        tiles_to(m, start, start + 16, n, across, ysem.at[m, part]).start()

    def c_send(m, start, n):
        tiles_to(m, start, start, n, sibling, csem.at[m]).start()

    def gather(m, e):
        def zero():
            if e == 0:
                z_send(m, 0, 0, 0)
                z_send(m, 1, 0, 0)
                y_send(m, 0, 2)
            elif e in (1, 2):
                z_wait(m, 2 * e - 1, 0)
                z_send(m, 0, 2 * e - 1, 0)
                z_wait(m, 2 * e, 0)
                z_send(m, 1, 2 * e, 0)
                y_send(m, 4 * e - 2, 4)
            elif e == 3:
                z_wait(m, 5, 0)
                z_send(m, 0, 5, 0)
                z_wait(m, 6, 0)
                y_send(m, 10, 4)
            elif e == 4:
                z_wait(m, 7, 0)
                y_send(m, 14, 2, 1)
                tiles_to(m, 14, 30, 2, diagonal, csem.at[m]).start()
                c_send(m, 0, 16)
            elif e == 5:
                tiles_to(m, 16, 16, 14, across, ysem.at[m, 0]).wait_recv()
                c_send(m, 16, 14)
            elif e == 6:
                tiles_to(m, 30, 30, 2, across, ysem.at[m, 1]).wait_recv()
                tiles_to(m, 32, 32, 32, sibling, csem.at[m]).wait_recv()

        def one():
            if e == 0:
                tiles_to(m, 32, 34, 2, across, ysem.at[m, 0]).start()
                tiles_to(m, 32, 36, 2, up, zsem.at[m, 1]).start()
                tiles_to(m, 32, 40, 2, down, zsem.at[m, 2]).start()
            elif e == 1:
                tiles_to(m, 34, 34, 2, across, ysem.at[m, 0]).wait_recv()
                tiles_to(m, 34, 38, 2, up, zsem.at[m, 1]).start()
                tiles_to(m, 34, 42, 2, down, zsem.at[m, 2]).start()
            elif e in (2, 3):
                z_wait(m, 2 * e - 3, 1)
                z_send(m, 0, 2 * e - 3, 1)
                z_wait(m, 2 * e - 2, 1)
                z_send(m, 1, 2 * e - 2, 1)
            elif e == 4:
                z_wait(m, 6, 1)
                z_send(m, 1, 6, 1)
                z_wait(m, 5, 1)
                c_send(m, 32, 28)
            elif e == 5:
                z_wait(m, 7, 1)
                c_send(m, 60, 4)
            elif e == 6:
                tiles_to(m, 0, 0, 32, sibling, csem.at[m]).wait_recv()

        pl.when(core == 0)(zero)
        pl.when(core == 1)(one)

    def multiply(m, hooks):
        M = CHUNKS[m]

        def step(b, run):
            for at, todo in hooks.items():

                @pl.when(b == at)
                def _():
                    for item in todo:
                        do(item)

            products, opens = [], []
            for q in range(BATCH):
                s = 2 * (b * BATCH + q)
                left = jnp.concatenate([G[m][meta[1, s]], G[m][meta[1, s + 1]]], axis=1)
                right = jnp.concatenate([tiles[meta[0, s]], tiles[meta[0, s + 1]]], axis=0)
                products.append(jnp.dot(left, right, preferred_element_type=jnp.float32))
                opens.append(meta[2, s])
            for q in range(BATCH):
                run = jnp.where(opens[q] != 0, 0.0, run) + products[q]
                sums[b * BATCH + q, :M] = run.astype(jnp.bfloat16)
            return run

        lax.fori_loop(0, PAIRS // BATCH, step, jnp.zeros((M, T), jnp.float32))

    def whole(ref, ssem, rsem):
        return pltpu.make_async_remote_copy(
            src_ref=ref, dst_ref=ref, send_sem=ssem, recv_sem=rsem, device_id=up, device_id_type=MESH
        )

    def hop(src, dst, ssem, rsem, to):
        return pltpu.make_async_remote_copy(
            src_ref=src, dst_ref=dst, send_sem=ssem, recv_sem=rsem, device_id=to, device_id_type=MESH
        )

    sides = ((0, x, along_x, y, along_y), (1, y, along_y, x, along_x))

    def reduce(m, e):
        M, H = CHUNKS[m], CHUNKS[m] // 2
        if e == 0:
            for c in range(32):
                v = sums[meta[3, c], :M]
                xd, yd, t = c // 8, c // 2 % 4, c % 2
                SB[m][xd, 2 * yd + t] = v[:H]
                SB[m][4 + yd, 2 * xd + t] = v[H:]
            for k in (1, 0, 2):
                for side, me, along, _, _ in sides:
                    block = 4 * side + lax.rem(me + k + 1, 4)
                    hop(SB[m].at[block], R1[m].at[3 * side + k], s1.at[m], rs1.at[m], along[k]).start()
        elif e == 1:
            whole(R1[m], s1.at[m], rs1.at[m]).wait_recv()
            for side, me, _, place, after in sides:
                total = SB[m][4 * side + me].astype(jnp.float32)
                for k in range(3):
                    total += R1[m][3 * side + k].astype(jnp.float32)
                for d in range(4):
                    SC[m][4 * side + d] = total[2 * d : 2 * d + 2].astype(jnp.bfloat16)
                for k in (1, 0, 2):
                    block = 4 * side + lax.rem(place + k + 1, 4)
                    hop(SC[m].at[block], R2[m].at[3 * side + k], s2.at[m], rs2.at[m], after[k]).start()
            for side, me, _, place, _ in sides:
                at = pl.ds(2 * place, 2)
                mine = SB[m][4 * side + me, at].astype(jnp.float32)
                for k in range(3):
                    mine += R1[m][3 * side + k, at].astype(jnp.float32)
                own[m][side] = mine
        elif e == 2:
            whole(R2[m], s2.at[m], rs2.at[m]).wait_recv()
            for side in range(2):
                total = own[m][side]
                for k in range(3):
                    total += R2[m][3 * side + k].astype(jnp.float32)
                out_ref[:, pl.ds(firsts[m] + side * H, H), :] = total

    def sent(m):
        tiles_to(m, 0, 0, 62, up, csem.at[m]).wait_send()
        whole(R1[m], s1.at[m], rs1.at[m]).wait_send()
        whole(R2[m], s2.at[m], rs2.at[m]).wait_send()

    def do(item):
        kind, m, e = item
        if kind == "g":
            gather(m, e)
        elif kind == "r":
            reduce(m, e)
        elif kind == "p":
            for load in loads[1:4]:
                load.wait()
            table[...] = prepare(rows[...].reshape(1, SLOTS), cols[...].reshape(1, SLOTS), count[0], z, rep)
            to_scalars.start()
        elif kind == "t":
            loads[4].start()
        elif kind == "o":
            own_part(m)
        elif kind == "w":
            to_scalars.wait()
            loads[4].wait()
        else:
            hooks = {}
            for at, what in e:
                hooks.setdefault(at, []).append(what)
            multiply(m, hooks)

    to_scalars = pltpu.make_async_copy(table, meta, local.at[5])
    for item in PLAN:
        do(item)
    for m in range(F):
        sent(m)


def body(grad_out, tile_vals, tile_rows, tile_cols, tile_counts):
    vmem, bf16 = pltpu.VMEM, jnp.bfloat16
    F = len(CHUNKS)
    anywhere = pl.BlockSpec(memory_space=pl.ANY)
    shares = pl.pallas_call(
        kernel,
        out_shape=jax.ShapeDtypeStruct((2, D, T), jnp.float32),
        in_specs=[anywhere] * 5,
        out_specs=pl.BlockSpec(memory_space=vmem),
        scratch_shapes=[
            vmem((D, D), jnp.float32),
            vmem((SLOTS,), jnp.int32),
            vmem((SLOTS,), jnp.int32),
            pltpu.SMEM((1,), jnp.int32),
            vmem((SLOTS + 1, T, T), bf16),
            vmem((8, 512), jnp.int32),
            pltpu.SMEM((8, 512), jnp.int32),
            vmem((PAIRS + 1, max(CHUNKS), T), bf16),
        ]
        + [vmem((64, M, T), bf16) for M in CHUNKS]
        + [vmem((8, 8, M // 2, T), bf16) for M in CHUNKS]
        + [vmem((6, 8, M // 2, T), bf16) for M in CHUNKS]
        + [vmem((8, 2, M // 2, T), bf16) for M in CHUNKS]
        + [vmem((6, 2, M // 2, T), bf16) for M in CHUNKS]
        + [vmem((2, 2, M // 2, T), jnp.float32) for M in CHUNKS]
        + [
            pltpu.SemaphoreType.DMA((7,)),
            pltpu.SemaphoreType.DMA((F, 8)),
            pltpu.SemaphoreType.DMA((F, 2)),
        ]
        + [pltpu.SemaphoreType.DMA((F,)) for _ in range(6)],
        compiler_params=pltpu.CompilerParams(
            collective_id=0, has_side_effects=True, vmem_limit_bytes=56 * 2**20
        ),
    )(grad_out, tile_vals, tile_rows, tile_cols, tile_counts)
    return jnp.transpose(shares, (0, 2, 1)).reshape(2 * T, D)


def solution(mesh):
    placed = (
        P(("row", "col", "rep"), None),
        P(("row", "col", "rep"), None, None),
        P(("row", "col", "rep")),
        P(("row", "col", "rep")),
        P(("row", "col", "rep")),
    )
    return jax.shard_map(
        body, mesh=mesh, in_specs=placed, out_specs=P(("col", "row", "rep"), None), check_vma=False
    )
```

```python
import functools

import jax
import jax.numpy as jnp
from jax import lax
from jax.experimental import pallas as pl
from jax.experimental.pallas import tpu as pltpu
from jax.sharding import PartitionSpec as P

MESH = pl.DeviceIdType.MESH
T = 128
D = 256
SLOTS = 384
PAIRS = 208
BATCH = 104
CHUNKS = (64, 96, 96)
PLAN = (
    [("g", 0, 0), ("o", 1, 0), ("g", 1, 0), ("g", 2, 0)]
    + [("g", 0, 1), ("g", 1, 1), ("g", 2, 1), ("t", 0, 0)]
    + [("g", 0, 2), ("g", 1, 2), ("g", 2, 2), ("p", 0, 0)]
    + [("g", 0, 3), ("g", 1, 3), ("g", 2, 3)]
    + [("g", 0, 4), ("g", 1, 4), ("g", 0, 5), ("g", 2, 4), ("w", 0, 0), ("g", 0, 6)]
    + [("m", 0, [(0, ("g", 1, 5)), (1, ("g", 2, 5))]), ("r", 0, 0), ("g", 1, 6)]
    + [("m", 1, []), ("r", 1, 0), ("g", 2, 6)]
    + [("m", 2, [(1, ("r", 0, 1))]), ("r", 2, 0)]
    + [("r", 0, 2), ("r", 1, 1), ("r", 2, 1), ("r", 1, 2), ("r", 2, 2)]
)
X, Y, Z = 4, 4, 8


def prepare(rows, cols, count, z, y):
    zs, cs, ys, ts = rows >> 3, (rows >> 2) & 1, (rows >> 1) & 1, rows & 1
    zrel = (zs - z + 8) & 7
    zslot = jnp.where(zrel < 4, 2 * zrel, jnp.where(zrel == 4, 7, 15 - 2 * zrel))
    yrel = (ys - y + 2) & 1
    place = jnp.where(cs == 0, yrel * 16 + zslot * 2 + ts, 32 + zslot * 4 + yrel * 2 + ts)

    lane = lax.broadcasted_iota(jnp.int32, (1, SLOTS), 1)
    colr = jnp.where(lane < count, cols, 64)

    def column(v):
        return jnp.transpose(jnp.broadcast_to(v, (T, SLOTS)))

    colc, placec = column(colr), column(place)
    slotc = lax.broadcasted_iota(jnp.int32, (SLOTS, T), 0)
    one, zero = jnp.int32(1), jnp.int32(0)
    lanes = lax.broadcasted_iota(jnp.int32, (SLOTS, T), 1)
    n_row = jnp.sum(jnp.where(colc == lanes, one, zero), axis=0, keepdims=True)
    pair_row = jnp.where(lax.broadcasted_iota(jnp.int32, (1, T), 1) < 32, (n_row + 1) >> 1, 0)
    pair_col = jnp.transpose(jnp.broadcast_to(pair_row, (T, T)))
    sub = lax.broadcasted_iota(jnp.int32, (T, T), 0)
    lan = lax.broadcasted_iota(jnp.int32, (T, T), 1)
    ends = jnp.sum(jnp.where(sub <= lan, pair_col, zero), axis=0, keepdims=True)
    starts = ends - pair_row
    last = jnp.where(pair_row > 0, ends - 1, PAIRS)
    wide = jnp.concatenate([colc] * (SLOTS // T), axis=1)
    si = lax.broadcasted_iota(jnp.int32, (SLOTS, SLOTS), 0)
    ti = lax.broadcasted_iota(jnp.int32, (SLOTS, SLOTS), 1)
    same = jnp.where((wide == colr) & (ti < si), 1.0, 0.0)
    rank = jnp.sum(same, axis=1, keepdims=True).astype(jnp.int32)
    mine = jnp.where(colc == lanes, jnp.broadcast_to(starts, (SLOTS, T)), zero)
    start = jnp.sum(mine.astype(jnp.float32), axis=1, keepdims=True).astype(jnp.int32)
    pos = jnp.where(colc[:, :1] < 32, 2 * start + rank, -1)
    opens = jnp.where(rank == 0, one, zero)
    parts = [[], [], []]
    for block in range(4):
        target = lanes + block * T
        hit = jnp.broadcast_to(pos, (SLOTS, T)) == target
        parts[0].append(SLOTS + jnp.sum(jnp.where(hit, slotc - SLOTS, zero), axis=0, keepdims=True))
        parts[1].append(jnp.sum(jnp.where(hit, placec, zero), axis=0, keepdims=True))
        parts[2].append(jnp.sum(jnp.where(hit, jnp.broadcast_to(opens, (SLOTS, T)), zero), axis=0, keepdims=True))
    out = [jnp.concatenate(p, axis=1) for p in parts]
    out.append(jnp.concatenate([last] * 4, axis=1))
    return jnp.concatenate(out + out, axis=0)


def kernel(grad_hbm, tiles_hbm, rows_hbm, cols_hbm, count_hbm, out_ref, *scratch):
    F = len(CHUNKS)
    it = iter(scratch)
    grad, rows, cols, count, tiles, table, meta, sums = (next(it) for _ in range(8))
    G = [next(it) for _ in range(F)]
    SB = [next(it) for _ in range(F)]
    R1 = [next(it) for _ in range(F)]
    SC = [next(it) for _ in range(F)]
    R2 = [next(it) for _ in range(F)]
    own = [next(it) for _ in range(F)]
    local, zsem, ysem, csem, gsend, s1, s2, rs1, rs2 = (next(it) for _ in range(9))

    row, col, rep = lax.axis_index("row"), lax.axis_index("col"), lax.axis_index("rep")
    x, y = row // 2, lax.rem(row, 2) * 2 + rep
    z, core = col // 2, lax.rem(col, 2)

    def device(x, y, z, core):
        return (x * 2 + y // 2, z * 2 + core, lax.rem(y, 2))

    up = device(x, y, lax.rem(z + 1, Z), core)
    down = device(x, y, lax.rem(z + Z - 1, Z), core)
    across = device(x, y + 1 - 2 * rep, z, core)
    sibling = device(x, y, z, 1 - core)
    diagonal = device(x, y + 1 - 2 * rep, z, 1 - core)
    along_x = [device(lax.rem(x + k, X), y, z, core) for k in range(1, X)]
    along_y = [device(x, lax.rem(y + k, Y), z, core) for k in range(1, Y)]

    barrier = pltpu.get_barrier_semaphore()
    for other in [up, down, sibling, diagonal] + along_x + along_y:
        pl.semaphore_signal(barrier, inc=1, device_id=other, device_id_type=MESH)

    loads = [
        pltpu.make_async_copy(grad_hbm.at[:, pl.ds(0, T)], grad.at[:, pl.ds(0, T)], local.at[0]),
        pltpu.make_async_copy(rows_hbm, rows, local.at[1]),
        pltpu.make_async_copy(cols_hbm, cols, local.at[2]),
        pltpu.make_async_copy(count_hbm, count, local.at[3]),
        pltpu.make_async_copy(tiles_hbm, tiles.at[pl.ds(0, SLOTS)], local.at[4]),
        pltpu.make_async_copy(grad_hbm.at[:, pl.ds(T, T)], grad.at[:, pl.ds(T, T)], local.at[6]),
    ]
    for i in (0, 5, 1, 2, 3):
        loads[i].start()
    tiles[SLOTS] = jnp.zeros((T, T), jnp.bfloat16)
    sums[PAIRS] = jnp.zeros(sums.shape[1:], jnp.bfloat16)

    base = core * 32
    firsts = [sum(CHUNKS[:m]) for m in range(F)]

    def own_part(half):
        loads[5 * half].wait()
        for t in range(2):
            flipped = jnp.transpose(grad[t * T : (t + 1) * T, half * T : (half + 1) * T]).astype(jnp.bfloat16)
            for m in range(F):
                start, stop = max(firsts[m], half * T), min(firsts[m] + CHUNKS[m], half * T + T)
                if start < stop:
                    G[m][base + t, start - firsts[m] : stop - firsts[m]] = flipped[start - half * T : stop - half * T]

    own_part(0)
    pl.semaphore_wait(barrier, 10)

    def tiles_to(m, start, stop, n, to, sem):
        return pltpu.make_async_remote_copy(
            src_ref=G[m].at[pl.ds(start, n)],
            dst_ref=G[m].at[pl.ds(stop, n)],
            send_sem=gsend.at[m],
            recv_sem=sem,
            device_id=to,
            device_id_type=MESH,
        )

    def z_send(m, which, k, c):
        to = up if which == 0 else down
        nxt = 7 if k in (5, 6) else (k + 2 if k else 1 + which)
        at, n = (2, 2) if c == 0 else (4, 4)
        off = 32 * c
        tiles_to(m, off + at * k, off + at * nxt, n, to, zsem.at[m, nxt]).start()

    def z_wait(m, k, c):
        n = 2 if c == 0 else 4
        at = 2 * k if c == 0 else 32 + 4 * k
        tiles_to(m, at, at, n, up, zsem.at[m, k]).wait_recv()

    def y_send(m, start, n, part=0):
        tiles_to(m, start, start + 16, n, across, ysem.at[m, part]).start()

    def c_send(m, start, n):
        tiles_to(m, start, start, n, sibling, csem.at[m]).start()

    def gather(m, e):
        def zero():
            if e == 0:
                z_send(m, 0, 0, 0)
                z_send(m, 1, 0, 0)
                y_send(m, 0, 2)
            elif e in (1, 2):
                z_wait(m, 2 * e - 1, 0)
                z_send(m, 0, 2 * e - 1, 0)
                z_wait(m, 2 * e, 0)
                z_send(m, 1, 2 * e, 0)
                y_send(m, 4 * e - 2, 4)
            elif e == 3:
                z_wait(m, 5, 0)
                z_send(m, 0, 5, 0)
                z_wait(m, 6, 0)
                y_send(m, 10, 4)
            elif e == 4:
                z_wait(m, 7, 0)
                y_send(m, 14, 2, 1)
                tiles_to(m, 14, 30, 2, diagonal, csem.at[m]).start()
                c_send(m, 0, 16)
            elif e == 5:
                tiles_to(m, 16, 16, 14, across, ysem.at[m, 0]).wait_recv()
                c_send(m, 16, 14)
            elif e == 6:
                tiles_to(m, 30, 30, 2, across, ysem.at[m, 1]).wait_recv()
                tiles_to(m, 32, 32, 32, sibling, csem.at[m]).wait_recv()

        def one():
            if e == 0:
                tiles_to(m, 32, 34, 2, across, ysem.at[m, 0]).start()
                tiles_to(m, 32, 36, 2, up, zsem.at[m, 1]).start()
                tiles_to(m, 32, 40, 2, down, zsem.at[m, 2]).start()
            elif e == 1:
                tiles_to(m, 34, 34, 2, across, ysem.at[m, 0]).wait_recv()
                tiles_to(m, 34, 38, 2, up, zsem.at[m, 1]).start()
                tiles_to(m, 34, 42, 2, down, zsem.at[m, 2]).start()
            elif e in (2, 3):
                z_wait(m, 2 * e - 3, 1)
                z_send(m, 0, 2 * e - 3, 1)
                z_wait(m, 2 * e - 2, 1)
                z_send(m, 1, 2 * e - 2, 1)
            elif e == 4:
                z_wait(m, 6, 1)
                z_send(m, 1, 6, 1)
                z_wait(m, 5, 1)
                c_send(m, 32, 28)
            elif e == 5:
                z_wait(m, 7, 1)
                c_send(m, 60, 4)
            elif e == 6:
                tiles_to(m, 0, 0, 32, sibling, csem.at[m]).wait_recv()

        pl.when(core == 0)(zero)
        pl.when(core == 1)(one)

    def multiply(m, hooks):
        M = CHUNKS[m]

        def step(b, run):
            for at, todo in hooks.items():

                @pl.when(b == at)
                def _():
                    for item in todo:
                        do(item)

            products, opens = [], []
            for q in range(BATCH):
                s = 2 * (b * BATCH + q)
                left = jnp.concatenate([G[m][meta[1, s]], G[m][meta[1, s + 1]]], axis=1)
                right = jnp.concatenate([tiles[meta[0, s]], tiles[meta[0, s + 1]]], axis=0)
                products.append(jnp.dot(left, right, preferred_element_type=jnp.float32))
                opens.append(meta[2, s])
            for q in range(BATCH):
                run = jnp.where(opens[q] != 0, 0.0, run) + products[q]
                sums[b * BATCH + q, :M] = run.astype(jnp.bfloat16)
            return run

        lax.fori_loop(0, PAIRS // BATCH, step, jnp.zeros((M, T), jnp.float32))

    def whole(ref, ssem, rsem):
        return pltpu.make_async_remote_copy(
            src_ref=ref, dst_ref=ref, send_sem=ssem, recv_sem=rsem, device_id=up, device_id_type=MESH
        )

    def hop(src, dst, ssem, rsem, to):
        return pltpu.make_async_remote_copy(
            src_ref=src, dst_ref=dst, send_sem=ssem, recv_sem=rsem, device_id=to, device_id_type=MESH
        )

    sides = ((0, x, along_x, y, along_y), (1, y, along_y, x, along_x))

    def reduce(m, e):
        M, H = CHUNKS[m], CHUNKS[m] // 2
        if e == 0:
            for side, me, along, _, _ in sides:
                for c in range(32):
                    xd, yd, t = c // 8, c // 2 % 4, c % 2
                    block, at = (xd, 2 * yd + t) if side == 0 else (4 + yd, 2 * xd + t)
                    SB[m][block, at] = sums[meta[3, c], side * H : (side + 1) * H]
                for k in (1, 0, 2):
                    block = 4 * side + lax.rem(me + k + 1, 4)
                    hop(SB[m].at[block], R1[m].at[3 * side + k], s1.at[m], rs1.at[m, side], along[k]).start()
        elif e == 1:
            for side, me, _, place, after in sides:
                whole(R1[m].at[pl.ds(3 * side, 3)], s1.at[m], rs1.at[m, side]).wait_recv()
                total = SB[m][4 * side + me].astype(jnp.float32)
                for k in range(3):
                    total += R1[m][3 * side + k].astype(jnp.float32)
                for d in range(4):
                    SC[m][4 * side + d] = total[2 * d : 2 * d + 2].astype(jnp.bfloat16)
                for k in (1, 0, 2):
                    block = 4 * side + lax.rem(place + k + 1, 4)
                    hop(SC[m].at[block], R2[m].at[3 * side + k], s2.at[m], rs2.at[m, side], after[k]).start()
            for side, me, _, place, _ in sides:
                at = pl.ds(2 * place, 2)
                mine = SB[m][4 * side + me, at].astype(jnp.float32)
                for k in range(3):
                    mine += R1[m][3 * side + k, at].astype(jnp.float32)
                own[m][side] = mine
        elif e == 2:
            for side in range(2):
                whole(R2[m].at[pl.ds(3 * side, 3)], s2.at[m], rs2.at[m, side]).wait_recv()
                total = own[m][side]
                for k in range(3):
                    total += R2[m][3 * side + k].astype(jnp.float32)
                out_ref[:, pl.ds(firsts[m] + side * H, H), :] = total

    def sent(m):
        tiles_to(m, 0, 0, 62, up, csem.at[m]).wait_send()
        whole(R1[m], s1.at[m], rs1.at[m, 0]).wait_send()
        whole(R2[m], s2.at[m], rs2.at[m, 0]).wait_send()

    def do(item):
        kind, m, e = item
        if kind == "g":
            gather(m, e)
        elif kind == "r":
            reduce(m, e)
        elif kind == "p":
            for load in loads[1:4]:
                load.wait()
            table[...] = prepare(rows[...].reshape(1, SLOTS), cols[...].reshape(1, SLOTS), count[0], z, rep)
            to_scalars.start()
        elif kind == "t":
            loads[4].start()
        elif kind == "o":
            own_part(m)
        elif kind == "w":
            to_scalars.wait()
            loads[4].wait()
        else:
            hooks = {}
            for at, what in e:
                hooks.setdefault(at, []).append(what)
            multiply(m, hooks)

    to_scalars = pltpu.make_async_copy(table, meta, local.at[5])
    for item in PLAN:
        do(item)
    for m in range(F):
        sent(m)


def body(grad_out, tile_vals, tile_rows, tile_cols, tile_counts):
    vmem, bf16 = pltpu.VMEM, jnp.bfloat16
    F = len(CHUNKS)
    anywhere = pl.BlockSpec(memory_space=pl.ANY)
    shares = pl.pallas_call(
        kernel,
        out_shape=jax.ShapeDtypeStruct((2, D, T), jnp.float32),
        in_specs=[anywhere] * 5,
        out_specs=pl.BlockSpec(memory_space=vmem),
        scratch_shapes=[
            vmem((D, D), jnp.float32),
            vmem((SLOTS,), jnp.int32),
            vmem((SLOTS,), jnp.int32),
            pltpu.SMEM((1,), jnp.int32),
            vmem((SLOTS + 1, T, T), bf16),
            vmem((8, 512), jnp.int32),
            pltpu.SMEM((8, 512), jnp.int32),
            vmem((PAIRS + 1, max(CHUNKS), T), bf16),
        ]
        + [vmem((64, M, T), bf16) for M in CHUNKS]
        + [vmem((8, 8, M // 2, T), bf16) for M in CHUNKS]
        + [vmem((6, 8, M // 2, T), bf16) for M in CHUNKS]
        + [vmem((8, 2, M // 2, T), bf16) for M in CHUNKS]
        + [vmem((6, 2, M // 2, T), bf16) for M in CHUNKS]
        + [vmem((2, 2, M // 2, T), jnp.float32) for M in CHUNKS]
        + [
            pltpu.SemaphoreType.DMA((7,)),
            pltpu.SemaphoreType.DMA((F, 8)),
            pltpu.SemaphoreType.DMA((F, 2)),
        ]
        + [pltpu.SemaphoreType.DMA((F,)) for _ in range(4)]
        + [pltpu.SemaphoreType.DMA((F, 2)) for _ in range(2)],
        compiler_params=pltpu.CompilerParams(
            collective_id=0, has_side_effects=True, vmem_limit_bytes=56 * 2**20
        ),
    )(grad_out, tile_vals, tile_rows, tile_cols, tile_counts)
    return jnp.transpose(shares, (0, 2, 1)).reshape(2 * T, D)


def solution(mesh):
    placed = (
        P(("row", "col", "rep"), None),
        P(("row", "col", "rep"), None, None),
        P(("row", "col", "rep")),
        P(("row", "col", "rep")),
        P(("row", "col", "rep")),
    )
    return jax.shard_map(
        body, mesh=mesh, in_specs=placed, out_specs=P(("col", "row", "rep"), None), check_vma=False
    )
```
